32 devices in a mesh: pipe: 4 (over y, core), expert: 4 (over z), dp: 2 (over x).
Axes of the slice: x: 2, y: 2, z: 4, core: 2. Of those that a mesh axis runs over, the one named last changes fastest.
Arguments:
- upstream: bfloat16 [4, 1024, 2048], P('pipe', ('expert', 'dp')), may hold values from -6 to 6
- section_inputs: bfloat16 [4, 1024, 2048], P('pipe', ('expert', 'dp')), may hold values from -6 to 6
- route_ids: int32 [4, 1024, 2], P('pipe', ('expert', 'dp')), may hold values from 0 to 3, all different within a row; in each aligned block of 128 rows (0 to 127, 128 to 255, ..., all dimensions but the last counted through in order) at most 72 rows name the same one
- router_weight: bfloat16 [4, 2048, 4], P('pipe'), may hold values from -0.125 to 0.125
- w_gate: bfloat16 [4, 4, 448, 2048], P('pipe', 'expert'), may hold values from -0.125 to 0.125
- w_up: bfloat16 [4, 4, 448, 2048], P('pipe', 'expert'), may hold values from -0.125 to 0.125
- w_down: bfloat16 [4, 4, 448, 2048], P('pipe', 'expert'), may hold values from -0.25 to 0.25
- saved_preacts: bfloat16 [4, 4, 576, 896], P('pipe', 'expert', 'dp'), may hold values from -6 to 6
Outputs:
- input_grad: bfloat16 [4, 1024, 2048], P('pipe', ('expert', 'dp'))
- router_grad: float32 [4, 2048, 4], P('pipe')
The draws below stay inside these ranges and needn't reach their ends.
Inputs may be any that keep to these rules, and one draw needn't show every extreme that they name: `route_ids`: each row names 2 different experts. Within the rows of one device no expert is named more than 72 times, and in some device's rows some expert is named exactly 72 times.
All inputs are finite; a program needn't handle non-finite values.
Results may differ from the reference program's by a relative error of at most 0.0058.
Values may be sent and summed in bfloat16 or wider, within the bound.
No kernel may reach another device: no remote copies, remote signals or barrier semaphores. Data moves between devices by JAX's collectives and lax.ppermute only.
A program may use at most 64 MiB of HBM per device.

```python
import math
import jax
import jax.numpy as jnp
import numpy as np
from jax import lax

D = 2048
FF_W = 448
TOP = 2
TOK_DEV = 128
EXPERTS = 4
CAP = 72
SLOTS = 288
SECTION_TOK = 1024
N_PIPE = 4
N_EXPERT = 4
N_DP = 2


def block_scale(stream_key, extent, split, least, largest):
    level, own = 1.0, jax.random.fold_in(stream_key, 6)
    for axis_at, parts in split:
        heights = jnp.exp(jax.random.uniform(jax.random.fold_in(own, axis_at), (parts,), jnp.float32, least / len(split), largest / len(split)))
        level = level * jnp.repeat(heights, extent[axis_at] // parts).reshape([-1 if axis == axis_at else 1 for axis in range(len(extent))])
    return level


def shared_out(rng, own, number, rows, number_of, top, bound, lean):
    sequence = jax.random.permutation(rng, number_of)
    packed, common = portions_of(number_of, rows * top, bound, lean, True), portions_of(number_of, rows * top, bound, lean, False)
    places = jnp.arange(number_of)

    def named(sizes, turn):
        used = int((sizes > 0).sum())
        fixed = max(1, used // 4)
        passed = fixed + (places - fixed + turn * (used - fixed)) % max(1, number_of - fixed)
        return jnp.zeros((number_of,), jnp.int32).at[sequence[jnp.where(places < fixed, places, passed)]].set(jnp.asarray(sizes, jnp.int32))

    sizes = jnp.where(number % 4 == 0, named(packed, number // 4), named(common, number - number // 4 - 1))
    mixed = jax.random.permutation(jax.random.fold_in(own, 3), number_of)
    source_of, receiver = mixed[0:number_of // 2 * 2:2], mixed[1:number_of // 2 * 2:2]
    slack = jnp.minimum(sizes[source_of] - 1, bound - sizes[receiver]) // 2
    slack = jnp.where((source_of == sequence[0]) | (receiver == sequence[0]) | (sizes[receiver] == 0), 0, jnp.maximum(slack, 0))
    passed = jax.random.randint(jax.random.fold_in(own, 4), (number_of // 2,), 0, 1 << 20) % (slack + 1)
    sizes = sizes.at[source_of].add(-passed).at[receiver].add(passed)
    items = jnp.searchsorted(jnp.cumsum(sizes), jnp.arange(rows * top), side="right").astype(jnp.int32)
    grid = items.reshape(top, rows).T
    grid = grid[jax.random.permutation(jax.random.fold_in(own, 1), rows)]
    turn = jax.random.randint(jax.random.fold_in(own, 2), (rows, 1), 0, top)
    return jnp.take_along_axis(grid, (jnp.arange(top)[None, :] + turn) % top, axis=1)


def portions_of(amount, total, limit, skew, full):
    weights = [(1 << 20) // math.isqrt(standing ** skew) + 1 for standing in range(1, amount + 1)]
    largest = limit if full else min(limit, max(-(-total // amount), total * weights[0] // sum(weights)))
    least = 1 if total - largest >= amount - 1 else 0
    given, spare = [largest] + [least] * (amount - 1), total - largest - least * (amount - 1)
    while spare > 0:
        free = [i for i in range(1, amount) if given[i] < largest] or [i for i in range(1, amount) if given[i] < limit]
        mass, left = sum([weights[i] for i in free]), spare
        for i in free:
            more = min(limit - given[i], max(1, left * weights[i] // mass), spare)
            given[i] = given[i] + more
            spare = spare - more
    return np.array(given)


def normal_values(rng, extent, deviation, bound, split=(), kind=jnp.bfloat16):
    factor_of = block_scale(rng, extent, split, -0.22, 0.18) if split else 1.0
    entries = jax.random.normal(rng, extent, jnp.float32) * deviation * factor_of
    return jnp.minimum(jnp.maximum(entries, -bound), bound).astype(kind)


def setup_inputs(seed: int = 0) -> dict:
    splits = jax.random.split(jax.random.key(seed), 9)
    upstream = normal_values(splits[0], (N_PIPE, SECTION_TOK, D), 1.0, 6.0, ((0, 4), (1, 8)))
    section_inputs = normal_values(splits[1], (N_PIPE, SECTION_TOK, D), 1.0, 6.0, ((0, 4), (1, 8)))
    route_ids_keys = jax.random.split(jax.random.fold_in(splits[2], 1), N_PIPE * SECTION_TOK // TOK_DEV)
    route_ids_turns = jax.random.permutation(jax.random.fold_in(splits[2], 3), N_PIPE * SECTION_TOK // TOK_DEV)
    route_ids = jax.vmap(lambda own, number: shared_out(jax.random.fold_in(splits[2], 2), own, number, TOK_DEV, EXPERTS, TOP, CAP, 2))(route_ids_keys, route_ids_turns).reshape((N_PIPE, SECTION_TOK, TOP))
    router_weight = normal_values(splits[3], (N_PIPE, D, EXPERTS), D ** -0.5, 0.125, ((0, 4),))
    w_gate = normal_values(splits[4], (N_PIPE, EXPERTS, FF_W, D), D ** -0.5, 0.125, ((0, 4), (1, 4)))
    w_up = normal_values(splits[5], (N_PIPE, EXPERTS, FF_W, D), D ** -0.5, 0.125, ((0, 4), (1, 4)))
    w_down = normal_values(splits[6], (N_PIPE, EXPERTS, FF_W, D), FF_W ** -0.5, 0.25, ((0, 4), (1, 4)))
    saved_preacts = normal_values(splits[7], (N_PIPE, EXPERTS, N_DP * SLOTS, 2 * FF_W), 1.0, 6.0, ((0, 4), (1, 4), (2, 2)))
    return {"upstream": upstream, "section_inputs": section_inputs, "route_ids": route_ids, "router_weight": router_weight, "w_gate": w_gate, "w_up": w_up, "w_down": w_down, "saved_preacts": saved_preacts}


def expert_backward(rows, preacts, w_gate, w_up, w_down):
    gate_pre = preacts[..., :FF_W].astype(jnp.float32)
    upper = preacts[..., FF_W:].astype(jnp.float32)
    hidden_grad = jnp.einsum('erd,efd->erf', rows.astype(jnp.float32), w_down.astype(jnp.float32))
    sig_gate = jax.nn.sigmoid(gate_pre)
    swish_val = gate_pre * sig_gate
    scores = lax.optimization_barrier(jnp.sum(hidden_grad * swish_val * upper, axis=-1)).astype(jnp.bfloat16)
    gate_grad = (hidden_grad * upper * sig_gate * (1.0 + gate_pre * (1.0 - sig_gate))).astype(jnp.bfloat16)
    upper_grad = (hidden_grad * swish_val).astype(jnp.bfloat16)
    rows_grad = jnp.einsum('erf,efd->erd', gate_grad.astype(jnp.float32), w_gate.astype(jnp.float32))
    rows_grad = rows_grad + jnp.einsum('erf,efd->erd', upper_grad.astype(jnp.float32), w_up.astype(jnp.float32))
    return (rows_grad.astype(jnp.bfloat16), scores)

def group_grad(grad_rows, inputs, routes, router, w_gate, w_up, w_down, preacts):
    sources = routes.shape[0]
    tokens = routes.shape[1]
    logits = jnp.einsum('std,de->ste', inputs.astype(jnp.float32), router.astype(jnp.float32))
    onehot = (routes[..., None] == jnp.arange(EXPERTS, dtype=jnp.int32)).astype(jnp.float32)
    chosen = lax.optimization_barrier(jnp.sum(logits[:, :, None, :] * onehot, axis=-1))
    first_prob = jax.nn.sigmoid(chosen[..., 0] - chosen[..., 1])
    second_prob = jax.nn.sigmoid(chosen[..., 1] - chosen[..., 0])
    gate_probs = jnp.stack([first_prob, second_prob], axis=-1)
    scaled = (gate_probs[..., None] * grad_rows[:, :, None, :].astype(jnp.float32)).astype(jnp.bfloat16)
    scaled = scaled.reshape(sources, tokens * TOP, D)
    flat_hits = onehot.reshape(sources, tokens * TOP, EXPERTS)
    earlier = jnp.cumsum(flat_hits, axis=1) - flat_hits
    position = lax.optimization_barrier(jnp.sum(earlier * flat_hits, axis=-1)).astype(jnp.int32)
    expert_id = routes.reshape(sources, tokens * TOP).astype(jnp.int32)
    source_id = jnp.broadcast_to(jnp.arange(sources, dtype=jnp.int32)[:, None], expert_id.shape)
    slots = jnp.zeros((EXPERTS, sources, CAP, D), jnp.bfloat16).at[expert_id, source_id, position].set(scaled)
    rows_grad, scores = expert_backward(slots.reshape(EXPERTS, sources * CAP, D), preacts, w_gate, w_up, w_down)
    rows_grad = rows_grad.reshape(EXPERTS, sources, CAP, D)
    scores = scores.reshape(EXPERTS, sources, CAP)
    back_rows = rows_grad[expert_id, source_id, position].astype(jnp.float32).reshape(sources, tokens, TOP, D)
    pair_scores = scores[expert_id, source_id, position].astype(jnp.float32).reshape(sources, tokens, TOP)
    mixture = lax.optimization_barrier(jnp.sum(back_rows, axis=2))
    score_sum = lax.optimization_barrier(jnp.sum(pair_scores, axis=-1, keepdims=True))
    logit_grad = lax.optimization_barrier(jnp.sum((pair_scores - gate_probs * score_sum)[..., None] * onehot, axis=2)).astype(jnp.bfloat16)
    through_router = jnp.einsum('ste,de->std', logit_grad.astype(jnp.float32), router.astype(jnp.float32))
    result = (grad_rows.astype(jnp.float32) + mixture + through_router).astype(jnp.bfloat16)
    partial_grad = jnp.einsum('std,ste->de', inputs.astype(jnp.float32), logit_grad.astype(jnp.float32))
    return (result, partial_grad)

def regroup(array_in):
    tail = array_in.shape[2:]
    shaped = array_in.reshape((N_PIPE, N_EXPERT, N_DP, TOK_DEV) + tail)
    return jnp.swapaxes(shaped, 1, 2).reshape((N_PIPE * N_DP, N_EXPERT, TOK_DEV) + tail)

def reference(upstream, section_inputs, route_ids, router_weight, w_gate, w_up, w_down, saved_preacts):
    incoming = jnp.roll(upstream, -1, axis=0)
    grad_groups = regroup(incoming)
    input_groups = regroup(section_inputs)
    route_groups = regroup(route_ids)
    pre_groups = saved_preacts.reshape(N_PIPE, EXPERTS, N_DP, SLOTS, 2 * FF_W)
    pre_groups = jnp.transpose(pre_groups, (0, 2, 1, 3, 4)).reshape(N_PIPE * N_DP, EXPERTS, SLOTS, 2 * FF_W)

    def one_group(index):
        section = index // N_DP
        return group_grad(grad_groups[index], input_groups[index], route_groups[index], router_weight[section], w_gate[section], w_up[section], w_down[section], pre_groups[index])
    results, partials = lax.map(one_group, jnp.arange(N_PIPE * N_DP, dtype=jnp.int32))
    results = results.reshape(N_PIPE, N_DP, N_EXPERT, TOK_DEV, D)
    input_grad = jnp.swapaxes(results, 1, 2).reshape(N_PIPE, SECTION_TOK, D)
    router_grad = lax.optimization_barrier(jnp.sum(partials.reshape(N_PIPE, N_DP, D, EXPERTS), axis=1)) / SECTION_TOK
    return (input_grad, router_grad)
```

```python
import functools

import jax
import jax.numpy as jnp
from jax import lax
from jax.experimental import pallas as pl
from jax.experimental.pallas import tpu as pltpu
from jax.sharding import PartitionSpec as P

F32 = jnp.float32
BF16 = jnp.bfloat16
VMEM = pl.BlockSpec(memory_space=pltpu.VMEM)
SMEM = pl.BlockSpec(memory_space=pltpu.SMEM)
LANES = 128


def call(kernel, out_shape, specs, flops, size):
    return pl.pallas_call(
        kernel,
        out_shape=out_shape,
        in_specs=specs,
        out_specs=jax.tree.map(lambda _: VMEM, out_shape),
        compiler_params=pltpu.CompilerParams(vmem_limit_bytes=40 * 1024 * 1024),
        cost_estimate=pl.CostEstimate(flops=flops, bytes_accessed=size, transcendentals=0),
    )


def exchanged(value, axis, distance):
    count = lax.axis_size(axis)
    return lax.ppermute(value, axis, [(at, at ^ distance) for at in range(count)])


def route_kernel(capacity, me_ref, inputs_ref, routes_ref, router_ref, meta_ref):
    tokens = inputs_ref.shape[0]
    experts = router_ref.shape[0]
    logits = lax.dot_general(
        router_ref[...], inputs_ref[...], (((1,), (1,)), ((), ())), preferred_element_type=F32
    )
    routes = routes_ref[...]
    expert = lax.broadcasted_iota(jnp.int32, (experts, tokens), 0)
    first = (expert == routes[0:1]).astype(F32)
    second = (expert == routes[1:2]).astype(F32)
    chosen_0 = jnp.sum(logits * first, axis=0, keepdims=True)
    chosen_1 = jnp.sum(logits * second, axis=0, keepdims=True)
    earlier = lax.broadcasted_iota(jnp.int32, (tokens, tokens), 0)
    later = lax.broadcasted_iota(jnp.int32, (tokens, tokens), 1)
    before = (earlier < later).astype(BF16)
    counts = jnp.dot((first + second).astype(BF16), before, preferred_element_type=F32)
    position_0 = jnp.sum(counts * first, axis=0, keepdims=True)
    position_1 = jnp.sum(counts * second, axis=0, keepdims=True)
    away = (routes ^ me_ref[0]).astype(F32) * float(capacity)
    meta_ref[0:1] = jax.nn.sigmoid(chosen_0 - chosen_1)
    meta_ref[1:2] = jax.nn.sigmoid(chosen_1 - chosen_0)
    meta_ref[2:3] = away[0:1] + position_0
    meta_ref[3:4] = away[1:2] + position_1
    meta_ref[4:6] = routes.astype(F32)
    meta_ref[6:8] = jnp.zeros((2, tokens), F32)


def slots_of(meta, away, capacity):
    tokens = meta.shape[1]
    rows = lax.broadcasted_iota(jnp.int32, (capacity, tokens), 0).astype(F32) + float(away * capacity)
    return rows == meta[2:3], rows == meta[3:4]


def pack_kernel(aways, meta_ref, incoming_ref, *out_refs):
    meta = meta_ref[...]
    incoming = incoming_ref[...]
    for away, out_ref in zip(aways, out_refs):
        first, second = slots_of(meta, away, out_ref.shape[0])
        pick = jnp.where(first | second, 1.0, 0.0).astype(BF16)
        weight = jnp.where(first, meta[0:1], 0.0) + jnp.where(second, meta[1:2], 0.0)
        weight = jnp.sum(weight, axis=1, keepdims=True)
        rows = jnp.dot(pick, incoming, preferred_element_type=F32)
        out_ref[...] = (rows * weight).astype(BF16)


def expert_kernel(aways, me_ref, pre_ref, gate_ref, up_ref, down_ref, *refs):
    count = len(aways)
    row_refs, out_refs, score_refs = refs[:count], refs[count : 2 * count], refs[2 * count :]
    capacity, width = row_refs[0].shape[0], gate_ref.shape[0]
    me = me_ref[0]
    rows = jnp.concatenate([ref[...].astype(F32) for ref in row_refs], axis=0).astype(BF16)
    pre = jnp.concatenate([pre_ref[me ^ away].astype(F32) for away in aways], axis=0)
    hidden = lax.dot_general(
        rows, down_ref[...], (((1,), (1,)), ((), ())), preferred_element_type=F32
    )
    gate, upper = pre[:, :width], pre[:, width:]
    sig = jax.nn.sigmoid(gate)
    swish = gate * sig
    scores = jnp.sum(hidden * swish * upper, axis=1, keepdims=True).astype(BF16)
    gate_grad = (hidden * upper * sig * (1.0 + gate * (1.0 - sig))).astype(BF16)
    up_grad = (hidden * swish).astype(BF16)
    grad = jnp.dot(gate_grad, gate_ref[...], preferred_element_type=F32)
    grad = grad + jnp.dot(up_grad, up_ref[...], preferred_element_type=F32)
    spread = jnp.broadcast_to(scores.astype(F32), (count * capacity, LANES))
    for at in range(count):
        part = slice(at * capacity, (at + 1) * capacity)
        out_refs[at][...] = grad[part].astype(BF16)
        score_refs[at][...] = spread[part].astype(BF16)


def logit_kernel(aways, meta_ref, inputs_ref, *refs):
    score_refs, grad_ref, partial_ref = refs[:-2], refs[-2], refs[-1]
    meta = meta_ref[...]
    tokens = meta.shape[1]
    pair_0 = jnp.zeros((1, tokens), F32)
    pair_1 = jnp.zeros((1, tokens), F32)
    for away, ref in zip(aways, score_refs):
        first, second = slots_of(meta, away, ref.shape[0])
        score = ref[...].astype(F32)[:, 0:1]
        pair_0 = pair_0 + jnp.sum(jnp.where(first, score, 0.0), axis=0, keepdims=True)
        pair_1 = pair_1 + jnp.sum(jnp.where(second, score, 0.0), axis=0, keepdims=True)
    total = pair_0 + pair_1
    experts = grad_ref.shape[0]
    expert = lax.broadcasted_iota(jnp.int32, (experts, tokens), 0).astype(F32)
    grad = jnp.where(expert == meta[4:5], pair_0 - meta[0:1] * total, 0.0)
    grad = grad + jnp.where(expert == meta[5:6], pair_1 - meta[1:2] * total, 0.0)
    grad = grad.astype(BF16)
    grad_ref[...] = grad
    partial_ref[...] = jnp.dot(grad, inputs_ref[...], preferred_element_type=F32)


def through_kernel(incoming_ref, grad_ref, router_ref, out_ref):
    out_ref[...] = incoming_ref[...].astype(F32) + lax.dot_general(
        grad_ref[...], router_ref[...], (((0,), (0,)), ((), ())), preferred_element_type=F32
    )


def combine_kernel(aways, meta_ref, base_ref, *refs):
    out_ref = refs[-1]
    meta = meta_ref[...]
    total = base_ref[...]
    for away, ref in zip(aways, refs):
        first, second = slots_of(meta, away, ref.shape[0])
        pick = jnp.where(first | second, 1.0, 0.0).astype(BF16)
        total = total + lax.dot_general(
            pick, ref[...], (((0,), (0,)), ((), ())), preferred_element_type=F32
        )
    out_ref[...] = total.astype(out_ref.dtype)


def shards(upstream, section_inputs, route_ids, router_weight, w_gate, w_up, w_down, saved_preacts):
    sections = lax.axis_size("pipe")
    sources = lax.axis_size("expert")
    replicas = lax.axis_size("dp")
    tokens, features = section_inputs.shape[1:]
    capacity = saved_preacts.shape[2] // sources
    hidden = w_gate.shape[2]
    me = lax.axis_index("expert").astype(jnp.int32).reshape(1)
    inputs = section_inputs[0]
    routes = route_ids[0].T
    router = router_weight[0].T
    experts = router.shape[0]
    gate, up, down = w_gate[0, 0], w_up[0, 0], w_down[0, 0]
    pre = saved_preacts[0, 0].reshape(sources, capacity, 2 * hidden)
    incoming = lax.ppermute(
        upstream[0], "pipe", [(at, (at - 1) % sections) for at in range(sections)]
    )
    block = jax.ShapeDtypeStruct((capacity, features), BF16)
    spread = jax.ShapeDtypeStruct((capacity, LANES), BF16)
    block_bytes = capacity * features * 2

    meta = call(
        functools.partial(route_kernel, capacity),
        jax.ShapeDtypeStruct((8, tokens), F32),
        [SMEM, VMEM, VMEM, VMEM],
        2 * tokens * features * 8,
        tokens * features * 2,
    )(me, inputs, routes, router)

    far = [sources // 2]
    rest = [away for away in range(sources - 1, 0, -1) if away not in far]
    groups = [far + [0], rest]

    rows = {}
    for aways in (far, rest + [0]):
        packed = call(
            functools.partial(pack_kernel, aways),
            [block] * len(aways),
            [VMEM, VMEM],
            2 * tokens * features * capacity * len(aways),
            tokens * features * 2 + block_bytes * len(aways),
        )(meta, incoming)
        for away, value in zip(aways, packed):
            rows[away] = exchanged(value, "expert", away) if away else value

    back, scores = {}, {}
    for aways in groups:
        count = len(aways)
        results = call(
            functools.partial(expert_kernel, aways),
            [block] * count + [spread] * count,
            [SMEM] + [VMEM] * (4 + count),
            6 * capacity * count * features * hidden,
            3 * features * hidden * 2 + 2 * count * block_bytes,
        )(me, pre, gate, up, down, *[rows[away] for away in aways])
        for away, value, score in zip(aways, results[:count], results[count:]):
            scores[away] = exchanged(score, "expert", away) if away else score
            back[away] = exchanged(value, "expert", away) if away else value

    order = list(range(sources))
    logit_grad, partial = call(
        functools.partial(logit_kernel, order),
        [
            jax.ShapeDtypeStruct((experts, tokens), BF16),
            jax.ShapeDtypeStruct((experts, features), F32),
        ],
        [VMEM] * (2 + sources),
        2 * tokens * features * 8,
        tokens * features * 2,
    )(meta, inputs, *[scores[away] for away in order])
    step = 1
    while step < replicas:
        partial = partial + exchanged(partial, "dp", step)
        step *= 2
    if sources <= 4:
        partial = partial + sum(exchanged(partial, "expert", away) for away in range(1, sources))
    else:
        step = 1
        while step < sources:
            partial = partial + exchanged(partial, "expert", step)
            step *= 2
    router_grad = (partial / (tokens * sources * replicas)).T

    total = jax.ShapeDtypeStruct((tokens, features), F32)
    base = call(
        through_kernel, total, [VMEM] * 3, 2 * tokens * features * 8, tokens * features * 6
    )(incoming, logit_grad, router)
    early = groups[0]
    base = call(
        functools.partial(combine_kernel, early),
        total,
        [VMEM] * (2 + len(early)),
        2 * tokens * features * capacity * len(early),
        tokens * features * 8 + block_bytes * len(early),
    )(meta, base, *[back[away] for away in early])
    late = groups[1]
    result = call(
        functools.partial(combine_kernel, late),
        jax.ShapeDtypeStruct((tokens, features), BF16),
        [VMEM] * (2 + len(late)),
        2 * tokens * features * capacity * len(late),
        tokens * features * 6 + block_bytes * len(late),
    )(meta, base, *[back[away] for away in late])
    return (result[None], router_grad[None])


def solution(mesh):
    in_specs = (
        P("pipe", ("expert", "dp"), None),
        P("pipe", ("expert", "dp"), None),
        P("pipe", ("expert", "dp"), None),
        P("pipe", None, None),
        P("pipe", "expert", None, None),
        P("pipe", "expert", None, None),
        P("pipe", "expert", None, None),
        P("pipe", "expert", "dp", None),
    )
    out_specs = (P("pipe", ("expert", "dp"), None), P("pipe", None, None))
    return jax.shard_map(shards, mesh=mesh, in_specs=in_specs, out_specs=out_specs, check_vma=False)
```

```python
import functools

import jax
import jax.numpy as jnp
from jax import lax
from jax.experimental import pallas as pl
from jax.experimental.pallas import tpu as pltpu
from jax.sharding import PartitionSpec as P

F32 = jnp.float32
BF16 = jnp.bfloat16
VMEM = pl.BlockSpec(memory_space=pltpu.VMEM)
ANY = pl.BlockSpec(memory_space=pl.ANY)
SMEM = pl.BlockSpec(memory_space=pltpu.SMEM)
LANES = 128


def call(kernel, out_shape, specs, flops, size):
    return pl.pallas_call(
        kernel,
        out_shape=out_shape,
        in_specs=specs,
        out_specs=jax.tree.map(lambda _: VMEM, out_shape),
        compiler_params=pltpu.CompilerParams(vmem_limit_bytes=40 * 1024 * 1024),
        cost_estimate=pl.CostEstimate(flops=flops, bytes_accessed=size, transcendentals=0),
    )


def exchanged(value, axis, distance):
    count = lax.axis_size(axis)
    return lax.ppermute(value, axis, [(at, at ^ distance) for at in range(count)])


def route_kernel(capacity, me_ref, inputs_ref, routes_ref, router_ref, meta_ref):
    tokens = inputs_ref.shape[0]
    experts = router_ref.shape[0]
    logits = lax.dot_general(
        router_ref[...], inputs_ref[...], (((1,), (1,)), ((), ())), preferred_element_type=F32
    )
    routes = routes_ref[...]
    expert = lax.broadcasted_iota(jnp.int32, (experts, tokens), 0)
    first = (expert == routes[0:1]).astype(F32)
    second = (expert == routes[1:2]).astype(F32)
    chosen_0 = jnp.sum(logits * first, axis=0, keepdims=True)
    chosen_1 = jnp.sum(logits * second, axis=0, keepdims=True)
    earlier = lax.broadcasted_iota(jnp.int32, (tokens, tokens), 0)
    later = lax.broadcasted_iota(jnp.int32, (tokens, tokens), 1)
    before = (earlier < later).astype(BF16)
    counts = jnp.dot((first + second).astype(BF16), before, preferred_element_type=F32)
    position_0 = jnp.sum(counts * first, axis=0, keepdims=True)
    position_1 = jnp.sum(counts * second, axis=0, keepdims=True)
    away = (routes ^ me_ref[0]).astype(F32) * float(capacity)
    meta_ref[0:1] = jax.nn.sigmoid(chosen_0 - chosen_1)
    meta_ref[1:2] = jax.nn.sigmoid(chosen_1 - chosen_0)
    meta_ref[2:3] = away[0:1] + position_0
    meta_ref[3:4] = away[1:2] + position_1
    meta_ref[4:6] = routes.astype(F32)
    meta_ref[6:8] = jnp.zeros((2, tokens), F32)


def slots_of(meta, away, capacity):
    tokens = meta.shape[1]
    rows = lax.broadcasted_iota(jnp.int32, (capacity, tokens), 0).astype(F32) + float(away * capacity)
    return rows == meta[2:3], rows == meta[3:4]


def packed_rows(meta, values, away, capacity):
    first, second = slots_of(meta, away, capacity)
    pick = jnp.where(first | second, 1.0, 0.0).astype(BF16)
    weight = jnp.where(first, meta[0:1], 0.0) + jnp.where(second, meta[1:2], 0.0)
    weight = jnp.sum(weight, axis=1, keepdims=True)
    rows = jnp.dot(pick, values, preferred_element_type=F32)
    return (rows * weight).astype(BF16)


def pack_kernel(whole, part, meta_ref, incoming_ref, *out_refs):
    meta = meta_ref[...]
    incoming = incoming_ref[...]
    for away, out_ref in zip(list(whole) + list(part), out_refs):
        capacity, width = out_ref.shape
        out_ref[...] = packed_rows(meta, incoming[:, incoming.shape[1] - width :], away, capacity)


def held_kernel(*refs):
    refs[-1][...] = refs[0][...]


def after_kernel(aways, _raw, _held, meta_ref, incoming_ref, *out_refs):
    pack_kernel([], aways, meta_ref, incoming_ref, *out_refs)


def relay_kernel(aways, _held, meta_ref, raw_ref, *out_refs):
    pack_kernel([], aways, meta_ref, raw_ref, *out_refs)


def swiglu_grads(rows, pre, gate_ref, up_ref, down_ref):
    width = gate_ref.shape[0]
    hidden = lax.dot_general(
        rows, down_ref[...], (((1,), (1,)), ((), ())), preferred_element_type=F32
    )
    gate, upper = pre[:, :width], pre[:, width:]
    sig = jax.nn.sigmoid(gate)
    swish = gate * sig
    scores = jnp.sum(hidden * swish * upper, axis=1, keepdims=True).astype(BF16)
    gate_grad = (hidden * upper * sig * (1.0 + gate * (1.0 - sig))).astype(BF16)
    up_grad = (hidden * swish).astype(BF16)
    grad = jnp.dot(gate_grad, gate_ref[...], preferred_element_type=F32)
    grad = grad + jnp.dot(up_grad, up_ref[...], preferred_element_type=F32)
    return grad, jnp.broadcast_to(scores.astype(F32), (rows.shape[0], LANES))


def first_kernel(
    aways, me_ref, pre_ref, gate_ref, up_ref, down_ref, meta_ref, raw_ref, tail_ref, *refs
):
    count = len(aways)
    row_refs, out_refs = refs[: count - 1], refs[count - 1 :]
    capacity = tail_ref.shape[0]
    me = me_ref[0]
    head = packed_rows(meta_ref[...], raw_ref[...], aways[-1], capacity).astype(F32)
    far = jnp.concatenate([head, tail_ref[...].astype(F32)], axis=1)
    rows = jnp.concatenate([ref[...].astype(F32) for ref in row_refs] + [far], axis=0).astype(BF16)
    pre = jnp.concatenate([pre_ref[me ^ away].astype(F32) for away in aways], axis=0)
    grad, spread = swiglu_grads(rows, pre, gate_ref, up_ref, down_ref)
    features = grad.shape[1]
    for at in range(count):
        part = slice(at * capacity, (at + 1) * capacity)
        out_refs[at][:, :features] = grad[part].astype(BF16)
        out_refs[at][:, features:] = spread[part].astype(BF16)


def last_kernel(aways, early, me_ref, pre_ref, gate_ref, up_ref, down_ref, _, *refs):
    count = len(aways)
    head_refs, tail_refs, out_refs = refs[:count], refs[count : 2 * count], refs[2 * count :]
    capacity = head_refs[0].shape[0]
    me = me_ref[0]
    rows = [
        jnp.concatenate([head[...].astype(F32), tail[...].astype(F32)], axis=1)
        for head, tail in zip(head_refs, tail_refs)
    ]
    rows = jnp.concatenate(rows, axis=0).astype(BF16)
    pre = jnp.concatenate([pre_ref[me ^ away].astype(F32) for away in aways], axis=0)
    grad, spread = swiglu_grads(rows, pre, gate_ref, up_ref, down_ref)
    for at in range(count):
        part = slice(at * capacity, (at + 1) * capacity)
        out_refs[at][:, :early] = grad[part, :early].astype(BF16)
        out_refs[at][:, early:] = spread[part].astype(BF16)
        out_refs[count + at][...] = grad[part, early:].astype(BF16)


def mixed_rows(meta, aways, refs, width):
    total = 0.0
    for away, ref in zip(aways, refs):
        first, second = slots_of(meta, away, ref.shape[0])
        pick = jnp.where(first | second, 1.0, 0.0).astype(BF16)
        total = total + lax.dot_general(
            pick, ref[:, :width], (((0,), (0,)), ((), ())), preferred_element_type=F32
        )
    return total


def logit_kernel(whole, last, meta_ref, inputs_ref, incoming_ref, router_ref, *refs):
    whole_refs, last_refs = refs[: len(whole)], refs[len(whole) : -2]
    partial_ref, base_ref = refs[-2], refs[-1]
    meta = meta_ref[...]
    tokens, features = incoming_ref.shape
    pair_0 = jnp.zeros((1, tokens), F32)
    pair_1 = jnp.zeros((1, tokens), F32)
    for away, ref in zip(list(whole) + list(last), refs[:-2]):
        capacity, width = ref.shape
        first, second = slots_of(meta, away, capacity)
        score = ref[:, width - LANES :].astype(F32)[:, 0:1]
        pair_0 = pair_0 + jnp.sum(jnp.where(first, score, 0.0), axis=0, keepdims=True)
        pair_1 = pair_1 + jnp.sum(jnp.where(second, score, 0.0), axis=0, keepdims=True)
    total = pair_0 + pair_1
    experts = router_ref.shape[0]
    expert = lax.broadcasted_iota(jnp.int32, (experts, tokens), 0).astype(F32)
    grad = jnp.where(expert == meta[4:5], pair_0 - meta[0:1] * total, 0.0)
    grad = grad + jnp.where(expert == meta[5:6], pair_1 - meta[1:2] * total, 0.0)
    grad = grad.astype(BF16)
    partial_ref[...] = jnp.dot(grad, inputs_ref[...], preferred_element_type=F32)
    through = lax.dot_general(
        grad, router_ref[...], (((0,), (0,)), ((), ())), preferred_element_type=F32
    )
    base = incoming_ref[...].astype(F32) + through + mixed_rows(meta, whole, whole_refs, features)
    split = last_refs[0].shape[1] - LANES
    base_ref[:, :split] = base[:, :split] + mixed_rows(meta, last, last_refs, split)
    base_ref[:, split:] = base[:, split:]


def final_kernel(aways, count, meta_ref, base_ref, *refs):
    out_ref, router_ref = refs[-2], refs[-1]
    width = refs[0].shape[1]
    split = out_ref.shape[1] - width
    out_ref[:, :split] = base_ref[:, :split].astype(out_ref.dtype)
    total = base_ref[:, split:] + mixed_rows(meta_ref[...], aways, refs[: len(aways)], width)
    out_ref[:, split:] = total.astype(out_ref.dtype)
    parts = [ref[...].astype(F32) for ref in refs[len(aways) : -2]]
    router_ref[...] = sum(parts[1:], parts[0]) / float(count)


def shards(upstream, section_inputs, route_ids, router_weight, w_gate, w_up, w_down, saved_preacts):
    sections = lax.axis_size("pipe")
    sources = lax.axis_size("expert")
    replicas = lax.axis_size("dp")
    tokens, features = section_inputs.shape[1:]
    capacity = saved_preacts.shape[2] // sources
    hidden = w_gate.shape[2]
    me = lax.axis_index("expert").astype(jnp.int32).reshape(1)
    inputs = section_inputs[0]
    routes = route_ids[0].T
    router = router_weight[0].T
    experts = router.shape[0]
    gate, up, down = w_gate[0, 0], w_up[0, 0], w_down[0, 0]
    pre = saved_preacts[0, 0].reshape(sources, capacity, 2 * hidden)
    half = sources // 2
    split = features * 5 // 8
    early = features * 11 // 16
    near, last = list(range(half)), list(range(half + 1, sources))

    def shape(rows, columns, kind=BF16):
        return jax.ShapeDtypeStruct((rows, columns), kind)

    block_bytes = capacity * features * 2
    weight_bytes = 3 * features * hidden * 2
    row_flops = 6 * capacity * features * hidden
    pick_flops = 2 * tokens * features * capacity

    earlier_section = [(at, (at - 1) % sections) for at in range(sections)]
    raw = lax.ppermute(
        upstream[0, :, :split],
        ("pipe", "expert"),
        [
            (source * sources + at, target * sources + (at ^ half))
            for source, target in earlier_section
            for at in range(sources)
        ],
    )
    incoming = lax.ppermute(upstream[0], "pipe", earlier_section)
    meta = call(
        functools.partial(route_kernel, capacity),
        shape(8, tokens, F32),
        [SMEM, VMEM, VMEM, VMEM],
        2 * tokens * features * 8,
        tokens * features * 2,
    )(me, inputs, routes, router)
    far_meta = exchanged(meta, "expert", half)

    packed = call(
        functools.partial(pack_kernel, near, [half]),
        [shape(capacity, features)] * half + [shape(capacity, features - split)],
        [VMEM, VMEM],
        pick_flops * (half + 1),
        tokens * features * 2 + block_bytes * (half + 1),
    )(meta, incoming)
    far_tail = exchanged(packed[half], "expert", half)
    rows = [exchanged(packed[away], "expert", away) if away else packed[0] for away in near]

    held = call(
        held_kernel, shape(8, tokens, F32), [VMEM] * 5 + [ANY], 0, 0
    )(meta, pre, gate, up, down, packed[0])
    late = call(
        functools.partial(after_kernel, last),
        [shape(capacity, features - split)] * len(last),
        [ANY] * 2 + [VMEM] * 2,
        pick_flops * len(last),
        tokens * features * 2 + block_bytes * len(last),
    )(raw, held, meta, incoming)
    relays = call(
        functools.partial(relay_kernel, last),
        [shape(capacity, split)] * len(last),
        [ANY] + [VMEM] * 2,
        pick_flops * len(last),
        tokens * features * 2 + block_bytes * len(last),
    )(held, far_meta, raw)
    tails = [exchanged(value, "expert", away) for away, value in zip(last, late)]
    heads = [exchanged(value, "expert", away - half) for away, value in zip(last, relays)]

    whole = near + [half]
    first = call(
        functools.partial(first_kernel, whole),
        [shape(capacity, features + LANES)] * len(whole),
        [SMEM] + [VMEM] * (7 + half),
        row_flops * len(whole),
        weight_bytes + 2 * block_bytes * len(whole),
    )(me, pre, gate, up, down, far_meta, raw, far_tail, *rows)
    back = [exchanged(value, "expert", away) if away else value for away, value in zip(whole, first)]

    ends = call(
        functools.partial(last_kernel, last, early),
        [shape(capacity, early + LANES)] * len(last) + [shape(capacity, features - early)] * len(last),
        [SMEM] + [VMEM] * 4 + [ANY] + [VMEM] * (2 * len(last)),
        row_flops * len(last),
        weight_bytes + 2 * block_bytes * len(last),
    )(me, pre, gate, up, down, first[0], *heads, *tails)
    back_heads = [exchanged(value, "expert", away) for away, value in zip(last, ends)]
    back_tails = [exchanged(value, "expert", away) for away, value in zip(last, ends[len(last) :])]

    partial, base = call(
        functools.partial(logit_kernel, whole, last),
        [shape(experts, features, F32), shape(tokens, features, F32)],
        [VMEM] * (4 + sources),
        pick_flops * sources,
        tokens * features * 8 + block_bytes * sources,
    )(meta, inputs, incoming, router, *back, *back_heads)
    step = 1
    while step < replicas:
        partial = partial + exchanged(partial, "dp", step)
        step *= 2
    step = 1
    while step < sources // 4:
        partial = partial + exchanged(partial, "expert", step)
        step *= 2
    sent = partial.astype(BF16)
    parts = [partial] + [exchanged(sent, "expert", away) for away in range(step, sources, step)]

    result, router_grad = call(
        functools.partial(final_kernel, last, tokens * sources * replicas),
        [shape(tokens, features), shape(experts, features, F32)],
        [VMEM] * (2 + len(last) + len(parts)),
        pick_flops * len(last),
        tokens * features * 6 + block_bytes * len(last),
    )(meta, base, *back_tails, *parts)
    return (result[None], router_grad.T[None])


def solution(mesh):
    in_specs = (
        P("pipe", ("expert", "dp"), None),
        P("pipe", ("expert", "dp"), None),
        P("pipe", ("expert", "dp"), None),
        P("pipe", None, None),
        P("pipe", "expert", None, None),
        P("pipe", "expert", None, None),
        P("pipe", "expert", None, None),
        P("pipe", "expert", "dp", None),
    )
    out_specs = (P("pipe", ("expert", "dp"), None), P("pipe", None, None))
    return jax.shard_map(shards, mesh=mesh, in_specs=in_specs, out_specs=out_specs, check_vma=False)
```

```python
import functools

import jax
import jax.numpy as jnp
from jax import lax
from jax.experimental import pallas as pl
from jax.experimental.pallas import tpu as pltpu
from jax.sharding import PartitionSpec as P

F32 = jnp.float32
BF16 = jnp.bfloat16
VMEM = pl.BlockSpec(memory_space=pltpu.VMEM)
ANY = pl.BlockSpec(memory_space=pl.ANY)
SMEM = pl.BlockSpec(memory_space=pltpu.SMEM)
LANES = 128
MARK = 16


def call(kernel, out_shape, specs, flops, size):
    return pl.pallas_call(
        kernel,
        out_shape=out_shape,
        in_specs=specs,
        out_specs=jax.tree.map(lambda _: VMEM, out_shape),
        compiler_params=pltpu.CompilerParams(vmem_limit_bytes=40 * 1024 * 1024),
        cost_estimate=pl.CostEstimate(flops=flops, bytes_accessed=size, transcendentals=0),
    )


def exchanged(value, axis, distance):
    count = lax.axis_size(axis)
    return lax.ppermute(value, axis, [(at, at ^ distance) for at in range(count)])


def route_kernel(capacity, me_ref, inputs_ref, routes_ref, router_ref, meta_ref):
    tokens = inputs_ref.shape[0]
    experts = router_ref.shape[0]
    logits = lax.dot_general(
        router_ref[...], inputs_ref[...], (((1,), (1,)), ((), ())), preferred_element_type=F32
    )
    routes = routes_ref[...]
    expert = lax.broadcasted_iota(jnp.int32, (experts, tokens), 0)
    first = (expert == routes[0:1]).astype(F32)
    second = (expert == routes[1:2]).astype(F32)
    chosen_0 = jnp.sum(logits * first, axis=0, keepdims=True)
    chosen_1 = jnp.sum(logits * second, axis=0, keepdims=True)
    earlier = lax.broadcasted_iota(jnp.int32, (tokens, tokens), 0)
    later = lax.broadcasted_iota(jnp.int32, (tokens, tokens), 1)
    before = (earlier < later).astype(BF16)
    counts = jnp.dot((first + second).astype(BF16), before, preferred_element_type=F32)
    position_0 = jnp.sum(counts * first, axis=0, keepdims=True)
    position_1 = jnp.sum(counts * second, axis=0, keepdims=True)
    away = (routes ^ me_ref[0]).astype(F32) * float(capacity)
    meta_ref[0:1] = jax.nn.sigmoid(chosen_0 - chosen_1)
    meta_ref[1:2] = jax.nn.sigmoid(chosen_1 - chosen_0)
    meta_ref[2:3] = away[0:1] + position_0
    meta_ref[3:4] = away[1:2] + position_1
    meta_ref[4:6] = routes.astype(F32)
    meta_ref[6:8] = jnp.zeros((2, tokens), F32)


def slots_of(meta, away, capacity):
    tokens = meta.shape[1]
    rows = lax.broadcasted_iota(jnp.int32, (capacity, tokens), 0).astype(F32) + float(away * capacity)
    return rows == meta[2:3], rows == meta[3:4]


def packed_rows(meta, values, away, capacity):
    first, second = slots_of(meta, away, capacity)
    pick = jnp.where(first | second, 1.0, 0.0).astype(BF16)
    weight = jnp.where(first, meta[0:1], 0.0) + jnp.where(second, meta[1:2], 0.0)
    weight = jnp.sum(weight, axis=1, keepdims=True)
    rows = jnp.dot(pick, values, preferred_element_type=F32)
    return (rows * weight).astype(BF16)


def pack_kernel(whole, part, meta_ref, incoming_ref, *out_refs):
    meta = meta_ref[...]
    incoming = incoming_ref[...]
    for away, out_ref in zip(list(whole) + list(part), out_refs):
        capacity, width = out_ref.shape
        out_ref[...] = packed_rows(meta, incoming[:, incoming.shape[1] - width :], away, capacity)


def held_kernel(*refs):
    refs[-1][...] = refs[0][...]


def after_kernel(aways, _raw, _held, meta_ref, incoming_ref, *out_refs):
    pack_kernel([], aways, meta_ref, incoming_ref, *out_refs)


def relay_kernel(aways, _held, meta_ref, raw_ref, *out_refs):
    pack_kernel([], aways, meta_ref, raw_ref, *out_refs)


def swiglu_grads(rows, pre, gate_ref, up_ref, down_ref):
    width = gate_ref.shape[0]
    hidden = lax.dot_general(
        rows, down_ref[...], (((1,), (1,)), ((), ())), preferred_element_type=F32
    )
    gate, upper = pre[:, :width], pre[:, width:]
    sig = jax.nn.sigmoid(gate)
    swish = gate * sig
    scores = jnp.sum(hidden * swish * upper, axis=1, keepdims=True).astype(BF16)
    gate_grad = (hidden * upper * sig * (1.0 + gate * (1.0 - sig))).astype(BF16)
    up_grad = (hidden * swish).astype(BF16)
    grad = jnp.dot(gate_grad, gate_ref[...], preferred_element_type=F32)
    grad = grad + jnp.dot(up_grad, up_ref[...], preferred_element_type=F32)
    return grad, jnp.broadcast_to(scores.astype(F32), (rows.shape[0], LANES))


def mark_of(width):
    return width % LANES or LANES


def written(aways, grad, spread, out_refs):
    out_refs = list(out_refs)
    features = grad.shape[1]
    for at in range(len(aways)):
        done = 0
        while done < features:
            ref = out_refs.pop(0)
            capacity, width = ref.shape
            part = slice(at * capacity, (at + 1) * capacity)
            if done == 0:
                mark = mark_of(width)
                width = width - mark
                ref[:, width:] = spread[part, :mark].astype(BF16)
            ref[:, :width] = grad[part, done : done + width].astype(BF16)
            done = done + width


def first_kernel(
    aways, me_ref, pre_ref, gate_ref, up_ref, down_ref, meta_ref, raw_ref, tail_ref, own_ref, *out_refs
):
    me = me_ref[0]
    capacity = tail_ref.shape[0]
    head = packed_rows(meta_ref[...], raw_ref[...], aways[-1], capacity).astype(F32)
    far = jnp.concatenate([head, tail_ref[...].astype(F32)], axis=1)
    rows = jnp.concatenate([own_ref[...].astype(F32), far], axis=0).astype(BF16)
    pre = jnp.concatenate([pre_ref[me ^ away].astype(F32) for away in aways], axis=0)
    grad, spread = swiglu_grads(rows, pre, gate_ref, up_ref, down_ref)
    written(aways, grad, spread, out_refs)


def last_kernel(aways, near, me_ref, pre_ref, gate_ref, up_ref, down_ref, _, *refs):
    me = me_ref[0]
    rows = [ref[...].astype(F32) for ref in refs[:near]]
    far = len(aways) - near
    for head, tail in zip(refs[near : near + far], refs[near + far : near + 2 * far]):
        rows.append(jnp.concatenate([head[...].astype(F32), tail[...].astype(F32)], axis=1))
    rows = jnp.concatenate(rows, axis=0).astype(BF16)
    pre = jnp.concatenate([pre_ref[me ^ away].astype(F32) for away in aways], axis=0)
    grad, spread = swiglu_grads(rows, pre, gate_ref, up_ref, down_ref)
    written(aways, grad, spread, refs[near + 2 * far :])


def mixed_rows(meta, away, values):
    first, second = slots_of(meta, away, values.shape[0])
    pick = jnp.where(first | second, 1.0, 0.0).astype(BF16)
    return lax.dot_general(pick, values, (((0,), (0,)), ((), ())), preferred_element_type=F32)


def logit_kernel(meta_ref, inputs_ref, incoming_ref, router_ref, *refs):
    head_refs, partial_ref, base_ref = refs[:-2], refs[-2], refs[-1]
    meta = meta_ref[...]
    tokens = meta.shape[1]
    pair_0 = jnp.zeros((1, tokens), F32)
    pair_1 = jnp.zeros((1, tokens), F32)
    for away, ref in enumerate(head_refs):
        capacity, width = ref.shape
        first, second = slots_of(meta, away, capacity)
        score = ref[:, width - mark_of(width) :].astype(F32)[:, 0:1]
        pair_0 = pair_0 + jnp.sum(jnp.where(first, score, 0.0), axis=0, keepdims=True)
        pair_1 = pair_1 + jnp.sum(jnp.where(second, score, 0.0), axis=0, keepdims=True)
    total = pair_0 + pair_1
    experts = router_ref.shape[0]
    expert = lax.broadcasted_iota(jnp.int32, (experts, tokens), 0).astype(F32)
    grad = jnp.where(expert == meta[4:5], pair_0 - meta[0:1] * total, 0.0)
    grad = grad + jnp.where(expert == meta[5:6], pair_1 - meta[1:2] * total, 0.0)
    grad = grad.astype(BF16)
    partial_ref[...] = jnp.dot(grad, inputs_ref[...], preferred_element_type=F32)
    through = lax.dot_general(
        grad, router_ref[...], (((0,), (0,)), ((), ())), preferred_element_type=F32
    )
    base_ref[...] = incoming_ref[...].astype(F32) + through
    for away, ref in enumerate(head_refs):
        width = ref.shape[1] - mark_of(ref.shape[1])
        base_ref[:, :width] += mixed_rows(meta, away, ref[:, :width])


def final_kernel(aways, count, meta_ref, base_ref, *refs):
    part_refs, (out_ref, router_ref) = refs[len(aways) : -2], refs[-2:]
    meta = meta_ref[...]
    done = out_ref.shape[1] - refs[0].shape[1]
    total = base_ref[:, done:]
    for away, ref in zip(aways, refs):
        total = total + mixed_rows(meta, away, ref[...])
    out_ref[:, :done] = base_ref[:, :done].astype(out_ref.dtype)
    out_ref[:, done:] = total.astype(out_ref.dtype)
    parts = [ref[...].astype(F32) for ref in part_refs]
    router_ref[...] = sum(parts[1:], parts[0]) / float(count)


def shards(upstream, section_inputs, route_ids, router_weight, w_gate, w_up, w_down, saved_preacts):
    sections = lax.axis_size("pipe")
    sources = lax.axis_size("expert")
    replicas = lax.axis_size("dp")
    tokens, features = section_inputs.shape[1:]
    capacity = saved_preacts.shape[2] // sources
    hidden = w_gate.shape[2]
    me = lax.axis_index("expert").astype(jnp.int32).reshape(1)
    inputs = section_inputs[0]
    routes = route_ids[0].T
    router = router_weight[0].T
    experts = router.shape[0]
    gate, up, down = w_gate[0, 0], w_up[0, 0], w_down[0, 0]
    pre = saved_preacts[0, 0].reshape(sources, capacity, 2 * hidden)
    half = sources // 2
    split = features * 5 // 8
    early = features * 7 // 16
    near, last = list(range(half)), list(range(half + 1, sources))

    def shape(rows, columns, kind=BF16):
        return jax.ShapeDtypeStruct((rows, columns), kind)

    block_bytes = capacity * features * 2
    weight_bytes = 3 * features * hidden * 2
    row_flops = 6 * capacity * features * hidden
    pick_flops = 2 * tokens * features * capacity

    earlier_section = [(at, (at - 1) % sections) for at in range(sections)]
    raw = lax.ppermute(
        upstream[0, :, :split],
        ("pipe", "expert"),
        [
            (source * sources + at, target * sources + (at ^ half))
            for source, target in earlier_section
            for at in range(sources)
        ],
    )
    incoming = lax.ppermute(upstream[0], "pipe", earlier_section)
    meta = call(
        functools.partial(route_kernel, capacity),
        shape(8, tokens, F32),
        [SMEM, VMEM, VMEM, VMEM],
        2 * tokens * features * 8,
        tokens * features * 2,
    )(me, inputs, routes, router)
    far_meta = exchanged(meta, "expert", half)

    packed = call(
        functools.partial(pack_kernel, near, [half]),
        [shape(capacity, features)] * half + [shape(capacity, features - split)],
        [VMEM, VMEM],
        pick_flops * (half + 1),
        tokens * features * 2 + block_bytes * (half + 1),
    )(meta, incoming)
    far_tail = exchanged(packed[half], "expert", half)
    rows = [exchanged(packed[away], "expert", away) if away else packed[0] for away in near]

    held = call(
        held_kernel, shape(8, tokens, F32), [VMEM] * 5 + [ANY], 0, 0
    )(meta, pre, gate, up, down, packed[0])
    late = call(
        functools.partial(after_kernel, last),
        [shape(capacity, features - split)] * len(last),
        [ANY] * 2 + [VMEM] * 2,
        pick_flops * len(last),
        tokens * features * 2 + block_bytes * len(last),
    )(raw, held, meta, incoming)
    relays = call(
        functools.partial(relay_kernel, last),
        [shape(capacity, split)] * len(last),
        [ANY] + [VMEM] * 2,
        pick_flops * len(last),
        tokens * features * 2 + block_bytes * len(last),
    )(held, far_meta, raw)
    tails_of_last = [exchanged(value, "expert", away) for away, value in zip(last, late)]
    relayed_heads = [exchanged(value, "expert", away - half) for away, value in zip(last, relays)]

    others = near[1:] + last

    def widths_of(away):
        if away > half:
            return [early + LANES, features - early]
        return [features + (MARK if 0 < away < half else LANES)]

    heads, tails = {}, {}

    def returned(aways, values):
        values = list(values)
        for away in aways:
            for width, into in zip(widths_of(away), (heads, tails)):
                value = values.pop(0)
                into[away] = exchanged(value, "expert", away) if away else value

    first = call(
        functools.partial(first_kernel, [0, half]),
        [shape(capacity, width) for away in (0, half) for width in widths_of(away)],
        [SMEM] + [VMEM] * 8,
        row_flops * 2,
        weight_bytes + 4 * block_bytes,
    )(me, pre, gate, up, down, far_meta, raw, far_tail, rows[0])
    returned([0, half], first)
    ends = call(
        functools.partial(last_kernel, others, half - 1),
        [shape(capacity, width) for away in others for width in widths_of(away)],
        [SMEM] + [VMEM] * 4 + [ANY] + [VMEM] * (half - 1 + 2 * len(last)),
        row_flops * len(others),
        weight_bytes + 2 * block_bytes * len(others),
    )(me, pre, gate, up, down, first[0], *rows[1:], *relayed_heads, *tails_of_last)
    returned(others, ends)

    partial, base = call(
        logit_kernel,
        [shape(experts, features, F32), shape(tokens, features, F32)],
        [VMEM] * (4 + sources),
        pick_flops * sources,
        tokens * features * 8 + block_bytes * sources,
    )(meta, inputs, incoming, router, *[heads[away] for away in range(sources)])
    step = 1
    while step < replicas:
        partial = partial + exchanged(partial, "dp", step)
        step *= 2
    step = 1
    while step < sources // 4:
        partial = partial + exchanged(partial, "expert", step)
        step *= 2
    sent = partial.astype(BF16)
    parts = [partial] + [exchanged(sent, "expert", away) for away in range(step, sources, step)]
    result, router_grad = call(
        functools.partial(final_kernel, sorted(tails), tokens * sources * replicas),
        [shape(tokens, features), shape(experts, features, F32)],
        [VMEM] * (2 + len(tails) + len(parts)),
        pick_flops * len(tails),
        tokens * features * 6 + block_bytes * len(tails),
    )(meta, base, *[tails[away] for away in sorted(tails)], *parts)
    return (result[None], router_grad.T[None])


def solution(mesh):
    in_specs = (
        P("pipe", ("expert", "dp"), None),
        P("pipe", ("expert", "dp"), None),
        P("pipe", ("expert", "dp"), None),
        P("pipe", None, None),
        P("pipe", "expert", None, None),
        P("pipe", "expert", None, None),
        P("pipe", "expert", None, None),
        P("pipe", "expert", "dp", None),
    )
    out_specs = (P("pipe", ("expert", "dp"), None), P("pipe", None, None))
    return jax.shard_map(shards, mesh=mesh, in_specs=in_specs, out_specs=out_specs, check_vma=False)
```

```python
import functools

import jax
import jax.numpy as jnp
from jax import lax
from jax.experimental import pallas as pl
from jax.experimental.pallas import tpu as pltpu
from jax.sharding import PartitionSpec as P

F32 = jnp.float32
BF16 = jnp.bfloat16
VMEM = pl.BlockSpec(memory_space=pltpu.VMEM)
ANY = pl.BlockSpec(memory_space=pl.ANY)
SMEM = pl.BlockSpec(memory_space=pltpu.SMEM)
LANES = 128
MARK = 16


def call(kernel, out_shape, specs, flops, size):
    return pl.pallas_call(
        kernel,
        out_shape=out_shape,
        in_specs=specs,
        out_specs=jax.tree.map(lambda _: VMEM, out_shape),
        compiler_params=pltpu.CompilerParams(vmem_limit_bytes=40 * 1024 * 1024),
        cost_estimate=pl.CostEstimate(flops=flops, bytes_accessed=size, transcendentals=0),
    )


def exchanged(value, axis, distance):
    count = lax.axis_size(axis)
    return lax.ppermute(value, axis, [(at, at ^ distance) for at in range(count)])


def route_kernel(capacity, me_ref, inputs_ref, routes_ref, router_ref, meta_ref):
    tokens = inputs_ref.shape[0]
    experts = router_ref.shape[0]
    logits = lax.dot_general(
        router_ref[...], inputs_ref[...], (((1,), (1,)), ((), ())), preferred_element_type=F32
    )
    routes = routes_ref[...]
    expert = lax.broadcasted_iota(jnp.int32, (experts, tokens), 0)
    first = (expert == routes[0:1]).astype(F32)
    second = (expert == routes[1:2]).astype(F32)
    chosen_0 = jnp.sum(logits * first, axis=0, keepdims=True)
    chosen_1 = jnp.sum(logits * second, axis=0, keepdims=True)
    earlier = lax.broadcasted_iota(jnp.int32, (tokens, tokens), 0)
    later = lax.broadcasted_iota(jnp.int32, (tokens, tokens), 1)
    before = (earlier < later).astype(BF16)
    counts = jnp.dot((first + second).astype(BF16), before, preferred_element_type=F32)
    position_0 = jnp.sum(counts * first, axis=0, keepdims=True)
    position_1 = jnp.sum(counts * second, axis=0, keepdims=True)
    away = (routes ^ me_ref[0]).astype(F32) * float(capacity)
    meta_ref[0:1] = jax.nn.sigmoid(chosen_0 - chosen_1)
    meta_ref[1:2] = jax.nn.sigmoid(chosen_1 - chosen_0)
    meta_ref[2:3] = away[0:1] + position_0
    meta_ref[3:4] = away[1:2] + position_1
    meta_ref[4:6] = routes.astype(F32)
    meta_ref[6:8] = jnp.zeros((2, tokens), F32)


def slots_of(meta, away, capacity):
    tokens = meta.shape[1]
    rows = lax.broadcasted_iota(jnp.int32, (capacity, tokens), 0).astype(F32) + float(away * capacity)
    return rows == meta[2:3], rows == meta[3:4]


def packed_rows(meta, values, away, capacity):
    first, second = slots_of(meta, away, capacity)
    pick = jnp.where(first | second, 1.0, 0.0).astype(BF16)
    weight = jnp.where(first, meta[0:1], 0.0) + jnp.where(second, meta[1:2], 0.0)
    weight = jnp.sum(weight, axis=1, keepdims=True)
    rows = jnp.dot(pick, values, preferred_element_type=F32)
    return (rows * weight).astype(BF16)


def pack_kernel(whole, part, meta_ref, incoming_ref, *out_refs):
    meta = meta_ref[...]
    incoming = incoming_ref[...]
    for away, out_ref in zip(list(whole) + list(part), out_refs):
        capacity, width = out_ref.shape
        out_ref[...] = packed_rows(meta, incoming[:, incoming.shape[1] - width :], away, capacity)


def held_kernel(*refs):
    refs[-1][...] = refs[0][...]


def after_kernel(aways, _raw, _held, meta_ref, incoming_ref, *out_refs):
    pack_kernel([], aways, meta_ref, incoming_ref, *out_refs)


def relay_kernel(aways, _held, meta_ref, raw_ref, *out_refs):
    pack_kernel([], aways, meta_ref, raw_ref, *out_refs)


def swiglu_grads(rows, pre, gate_ref, up_ref, down_ref):
    width = gate_ref.shape[0]
    hidden = lax.dot_general(
        rows, down_ref[...], (((1,), (1,)), ((), ())), preferred_element_type=F32
    )
    gate, upper = pre[:, :width], pre[:, width:]
    sig = jax.nn.sigmoid(gate)
    swish = gate * sig
    scores = jnp.sum(hidden * swish * upper, axis=1, keepdims=True).astype(BF16)
    gate_grad = (hidden * upper * sig * (1.0 + gate * (1.0 - sig))).astype(BF16)
    up_grad = (hidden * swish).astype(BF16)
    grad = jnp.dot(gate_grad, gate_ref[...], preferred_element_type=F32)
    grad = grad + jnp.dot(up_grad, up_ref[...], preferred_element_type=F32)
    return grad, jnp.broadcast_to(scores.astype(F32), (rows.shape[0], LANES))


def mark_of(width):
    return width % LANES or LANES


def written(aways, grad, spread, out_refs):
    out_refs = list(out_refs)
    features = grad.shape[1]
    for at in range(len(aways)):
        done = 0
        while done < features:
            ref = out_refs.pop(0)
            capacity, width = ref.shape
            part = slice(at * capacity, (at + 1) * capacity)
            if done == 0:
                mark = mark_of(width)
                width = width - mark
                ref[:, width:] = spread[part, :mark].astype(BF16)
            ref[:, :width] = grad[part, done : done + width].astype(BF16)
            done = done + width


def first_kernel(
    aways, me_ref, pre_ref, gate_ref, up_ref, down_ref, meta_ref, raw_ref, tail_ref, own_ref, *out_refs
):
    me = me_ref[0]
    capacity = tail_ref.shape[0]
    head = packed_rows(meta_ref[...], raw_ref[...], aways[-1], capacity).astype(F32)
    far = jnp.concatenate([head, tail_ref[...].astype(F32)], axis=1)
    rows = jnp.concatenate([own_ref[...].astype(F32), far], axis=0).astype(BF16)
    pre = jnp.concatenate([pre_ref[me ^ away].astype(F32) for away in aways], axis=0)
    grad, spread = swiglu_grads(rows, pre, gate_ref, up_ref, down_ref)
    written(aways, grad, spread, out_refs)


def last_kernel(aways, near, me_ref, pre_ref, gate_ref, up_ref, down_ref, _, *refs):
    me = me_ref[0]
    rows = [ref[...].astype(F32) for ref in refs[:near]]
    far = len(aways) - near
    for head, tail in zip(refs[near : near + far], refs[near + far : near + 2 * far]):
        rows.append(jnp.concatenate([head[...].astype(F32), tail[...].astype(F32)], axis=1))
    rows = jnp.concatenate(rows, axis=0).astype(BF16)
    pre = jnp.concatenate([pre_ref[me ^ away].astype(F32) for away in aways], axis=0)
    grad, spread = swiglu_grads(rows, pre, gate_ref, up_ref, down_ref)
    written(aways, grad, spread, refs[near + 2 * far :])


def mixed_rows(meta, away, values):
    first, second = slots_of(meta, away, values.shape[0])
    pick = jnp.where(first | second, 1.0, 0.0).astype(BF16)
    return lax.dot_general(pick, values, (((0,), (0,)), ((), ())), preferred_element_type=F32)


def logit_kernel(meta_ref, inputs_ref, incoming_ref, router_ref, *refs):
    head_refs, partial_ref, base_ref = refs[:-2], refs[-2], refs[-1]
    meta = meta_ref[...]
    tokens = meta.shape[1]
    pair_0 = jnp.zeros((1, tokens), F32)
    pair_1 = jnp.zeros((1, tokens), F32)
    for away, ref in enumerate(head_refs):
        capacity, width = ref.shape
        first, second = slots_of(meta, away, capacity)
        score = ref[:, width - mark_of(width) :].astype(F32)[:, 0:1]
        pair_0 = pair_0 + jnp.sum(jnp.where(first, score, 0.0), axis=0, keepdims=True)
        pair_1 = pair_1 + jnp.sum(jnp.where(second, score, 0.0), axis=0, keepdims=True)
    total = pair_0 + pair_1
    experts = router_ref.shape[0]
    expert = lax.broadcasted_iota(jnp.int32, (experts, tokens), 0).astype(F32)
    grad = jnp.where(expert == meta[4:5], pair_0 - meta[0:1] * total, 0.0)
    grad = grad + jnp.where(expert == meta[5:6], pair_1 - meta[1:2] * total, 0.0)
    grad = grad.astype(BF16)
    partial_ref[...] = jnp.dot(grad, inputs_ref[...], preferred_element_type=F32)
    through = lax.dot_general(
        grad, router_ref[...], (((0,), (0,)), ((), ())), preferred_element_type=F32
    )
    base_ref[...] = incoming_ref[...].astype(F32) + through
    for away, ref in enumerate(head_refs):
        width = ref.shape[1] - mark_of(ref.shape[1])
        base_ref[:, :width] += mixed_rows(meta, away, ref[:, :width])


def final_kernel(aways, count, meta_ref, base_ref, *refs):
    part_refs, (out_ref, router_ref) = refs[len(aways) : -2], refs[-2:]
    meta = meta_ref[...]
    done = out_ref.shape[1] - refs[0].shape[1]
    total = base_ref[:, done:]
    for away, ref in zip(aways, refs):
        total = total + mixed_rows(meta, away, ref[...])
    out_ref[:, :done] = base_ref[:, :done].astype(out_ref.dtype)
    out_ref[:, done:] = total.astype(out_ref.dtype)
    parts = [ref[...].astype(F32) for ref in part_refs]
    router_ref[...] = sum(parts[1:], parts[0]) / float(count)


def shards(upstream, section_inputs, route_ids, router_weight, w_gate, w_up, w_down, saved_preacts):
    sections = lax.axis_size("pipe")
    sources = lax.axis_size("expert")
    replicas = lax.axis_size("dp")
    tokens, features = section_inputs.shape[1:]
    capacity = saved_preacts.shape[2] // sources
    hidden = w_gate.shape[2]
    me = lax.axis_index("expert").astype(jnp.int32).reshape(1)
    inputs = section_inputs[0]
    routes = route_ids[0].T
    router = router_weight[0].T
    experts = router.shape[0]
    gate, up, down = w_gate[0, 0], w_up[0, 0], w_down[0, 0]
    pre = saved_preacts[0, 0].reshape(sources, capacity, 2 * hidden)
    half = sources // 2
    split = features * 5 // 8
    early = features * 9 // 16
    near, last = list(range(half)), list(range(half + 1, sources))

    def shape(rows, columns, kind=BF16):
        return jax.ShapeDtypeStruct((rows, columns), kind)

    block_bytes = capacity * features * 2
    weight_bytes = 3 * features * hidden * 2
    row_flops = 6 * capacity * features * hidden
    pick_flops = 2 * tokens * features * capacity

    earlier_section = [(at, (at - 1) % sections) for at in range(sections)]
    raw = lax.ppermute(
        upstream[0, :, :split],
        ("pipe", "expert"),
        [
            (source * sources + at, target * sources + (at ^ half))
            for source, target in earlier_section
            for at in range(sources)
        ],
    )
    incoming = lax.ppermute(upstream[0], "pipe", earlier_section)
    meta = call(
        functools.partial(route_kernel, capacity),
        shape(8, tokens, F32),
        [SMEM, VMEM, VMEM, VMEM],
        2 * tokens * features * 8,
        tokens * features * 2,
    )(me, inputs, routes, router)
    far_meta = exchanged(meta, "expert", half)

    packed = call(
        functools.partial(pack_kernel, near, [half]),
        [shape(capacity, features)] * half + [shape(capacity, features - split)],
        [VMEM, VMEM],
        pick_flops * (half + 1),
        tokens * features * 2 + block_bytes * (half + 1),
    )(meta, incoming)
    far_tail = exchanged(packed[half], "expert", half)
    rows = [exchanged(packed[away], "expert", away) if away else packed[0] for away in near]

    held = call(
        held_kernel, shape(8, tokens, F32), [VMEM] * 5 + [ANY], 0, 0
    )(meta, pre, gate, up, down, packed[0])
    late = call(
        functools.partial(after_kernel, last),
        [shape(capacity, features - split)] * len(last),
        [ANY] * 2 + [VMEM] * 2,
        pick_flops * len(last),
        tokens * features * 2 + block_bytes * len(last),
    )(raw, held, meta, incoming)
    relays = call(
        functools.partial(relay_kernel, last),
        [shape(capacity, split)] * len(last),
        [ANY] + [VMEM] * 2,
        pick_flops * len(last),
        tokens * features * 2 + block_bytes * len(last),
    )(held, far_meta, raw)
    tails_of_last = [exchanged(value, "expert", away) for away, value in zip(last, late)]
    relayed_heads = [exchanged(value, "expert", away - half) for away, value in zip(last, relays)]


    def widths_of(away):
        if away > half:
            return [early + LANES, features - early]
        return [features + (MARK if 0 < away < half else LANES)]

    heads, tails = {}, {}

    def returned(aways, values):
        values = list(values)
        for away in aways:
            for width, into in zip(widths_of(away), (heads, tails)):
                value = values.pop(0)
                into[away] = exchanged(value, "expert", away) if away else value

    first = call(
        functools.partial(first_kernel, [0, half]),
        [shape(capacity, width) for away in (0, half) for width in widths_of(away)],
        [SMEM] + [VMEM] * 8,
        row_flops * 2,
        weight_bytes + 4 * block_bytes,
    )(me, pre, gate, up, down, far_meta, raw, far_tail, rows[0])
    returned([0, half], first)
    before = first[0]
    for aways, near_count, values in (
        (near[1:], half - 1, rows[1:]),
        (last, 0, relayed_heads + tails_of_last),
    ):
        ends = call(
            functools.partial(last_kernel, aways, near_count),
            [shape(capacity, width) for away in aways for width in widths_of(away)],
            [SMEM] + [VMEM] * 4 + [ANY] + [VMEM] * len(values),
            row_flops * len(aways),
            weight_bytes + 2 * block_bytes * len(aways),
        )(me, pre, gate, up, down, before, *values)
        returned(aways, ends)
        before = ends[0]

    partial, base = call(
        logit_kernel,
        [shape(experts, features, F32), shape(tokens, features, F32)],
        [VMEM] * (4 + sources),
        pick_flops * sources,
        tokens * features * 8 + block_bytes * sources,
    )(meta, inputs, incoming, router, *[heads[away] for away in range(sources)])
    step = 1
    while step < replicas:
        partial = partial + exchanged(partial, "dp", step)
        step *= 2
    step = 1
    while step < sources // 4:
        partial = partial + exchanged(partial, "expert", step)
        step *= 2
    sent = partial.astype(BF16)
    parts = [partial] + [exchanged(sent, "expert", away) for away in range(step, sources, step)]
    result, router_grad = call(
        functools.partial(final_kernel, sorted(tails), tokens * sources * replicas),
        [shape(tokens, features), shape(experts, features, F32)],
        [VMEM] * (2 + len(tails) + len(parts)),
        pick_flops * len(tails),
        tokens * features * 6 + block_bytes * len(tails),
    )(meta, base, *[tails[away] for away in sorted(tails)], *parts)
    return (result[None], router_grad.T[None])


def solution(mesh):
    in_specs = (
        P("pipe", ("expert", "dp"), None),
        P("pipe", ("expert", "dp"), None),
        P("pipe", ("expert", "dp"), None),
        P("pipe", None, None),
        P("pipe", "expert", None, None),
        P("pipe", "expert", None, None),
        P("pipe", "expert", None, None),
        P("pipe", "expert", "dp", None),
    )
    out_specs = (P("pipe", ("expert", "dp"), None), P("pipe", None, None))
    return jax.shard_map(shards, mesh=mesh, in_specs=in_specs, out_specs=out_specs, check_vma=False)
```
